32 devices in a mesh: groups: 2 (over x), tensor: 16 (over z, y, core).
Axes of the slice: x: 2, y: 2, z: 4, core: 2. Of those that a mesh axis runs over, the one named last changes fastest.
Arguments:
- tokens: bfloat16 [4096, 6144], P(('groups', 'tensor')), parts along dimension 0, may hold values from -6 to 6
- expert_ids: int32 [4096, 4], P(('groups', 'tensor')), parts along dimension 0, may hold values from 0 to 15, as said below
- gates: float32 [4096, 4], P(('groups', 'tensor')), parts along dimension 0, may hold values from 0.2 to 1
- gate_weight: bfloat16 [10752, 6144], P('tensor'), may hold values from -0.078125 to 0.078125
- up_weight: bfloat16 [10752, 6144], P('tensor'), may hold values from -0.078125 to 0.078125
- down_weight: bfloat16 [10752, 6144], P('tensor'), may hold values from -0.078125 to 0.078125
Outputs:
- mixed: bfloat16 [4096, 6144], P(('groups', 'tensor')), parts along dimension 0
The draws below stay inside these ranges and needn't reach their ends.
There are 2 independent parts, one for each index of `groups`. The reference program is written for one: setup_inputs(seed, part) draws one part's arguments, and reference() takes and returns one part's arrays. A program takes and returns all parts, laid end to end along the dimension named above; an argument that names none is the same for every part. Nothing has to cross between parts.
Inputs may be any that keep to these rules, and one draw needn't show every extreme that they name: `expert_ids`: each row names 4 different experts. In every block of 128 rows of one index of tensor, expert 0 is named by 2 to 12 rows, and by exactly 12 rows in at least one block.
All inputs are finite; a program needn't handle non-finite values.
Results may differ from the reference program's by a relative error of at most 0.0085.
Values may be sent and summed in bfloat16 or wider, within the bound.
No kernel may reach another device: no remote copies, remote signals or barrier semaphores. Data moves between devices by JAX's collectives and lax.ppermute only.
A program may use at most 128 MiB of HBM per device.

```python
import jax
import jax.numpy as jnp
from jax import lax

D = 6144
FF = 10752
EXPERTS = 16
TOP = 4
TOK_DEV = 128
CAP = 12
TOKENS = 2048
N_TENSOR = 16


def draw_expert_ids(key, part):
    key = jax.random.fold_in(key, 11)
    keys = jax.random.split(key, 5)
    blocks = TOKENS // TOK_DEV
    counts = jax.random.randint(keys[0], (blocks,), 2, CAP + 1)
    full_block = jax.random.randint(keys[1], (), 0, blocks)
    counts = jnp.where(jnp.arange(blocks) == full_block, CAP, counts)
    block_keys = jax.random.split(keys[2], blocks)
    row_ranks = jax.vmap(lambda k: jax.random.permutation(k, TOK_DEV))(block_keys)
    chosen = (row_ranks < counts[:, None]).reshape(TOKENS)
    token_keys = jax.random.split(keys[3], TOKENS)
    others = jax.vmap(lambda k: jax.random.permutation(k, EXPERTS - 1))(token_keys)[:, :TOP] + 1
    column = jax.random.randint(keys[4], (TOKENS,), 0, TOP)
    placed = chosen[:, None] & (jnp.arange(TOP)[None, :] == column[:, None])
    return jnp.where(placed, 0, others).astype(jnp.int32)


def strengthened(array, key, source, target, blocks, factor):
    def block_of(dim):
        return (jnp.arange(array.shape[dim]) // (array.shape[dim] // blocks)).reshape((-1,) + (1,) * (array.ndim - 1 - dim))

    near = jax.random.permutation(key, blocks)[block_of(target)]
    other_side = (block_of(target) + blocks // 2) % blocks
    return jnp.where((block_of(source) == near) | (block_of(source) == other_side), factor * array, array)


def shard_levels(key, extent, shards, smallest, high):
    def one(position, blocks):
        heights = jax.random.uniform(jax.random.fold_in(jax.random.fold_in(key, 6), position), (blocks,), jnp.float32, smallest / len(shards), high / len(shards))
        return jnp.repeat(jnp.exp(heights), extent[position] // blocks).reshape((-1,) + (1,) * (len(extent) - position - 1))

    factor_of = one(*shards[0])
    for cut in shards[1:]:
        factor_of = factor_of * one(*cut)
    return factor_of


def normal_values(stream_key, shape, scale, limit, cuts=(), kind=jnp.bfloat16):
    result = jax.random.normal(stream_key, shape, jnp.float32) * scale
    if len(cuts) > 0:
        result = shard_levels(stream_key, shape, cuts, -0.22, 0.18) * result
    return jnp.clip(result, min=-limit, max=limit).astype(kind)


def noise_with(stream_key, dims, scale, limit, shards, heavy, kind=jnp.bfloat16):
    array = scale * jax.random.normal(stream_key, dims, jnp.float32)
    if shards:
        array = array * shard_levels(stream_key, dims, shards, -0.22, 0.18)
    return jnp.clip(strengthened(array, jax.random.fold_in(stream_key, 3), *heavy), -limit, limit).astype(kind)


def setup_inputs(seed: int = 0, part: int = 0) -> dict:
    key_of = jax.random.split(jax.random.key(seed), 7)
    part_splits = jax.random.split(jax.random.fold_in(key_of[6], part), 7)
    tokens = normal_values(part_splits[0], (TOKENS, D), 1.0, 6.0, ((0, 16),))
    expert_ids = draw_expert_ids(jax.random.fold_in(jax.random.fold_in(key_of[6], part), 71), part)
    gates = jnp.clip(0.2 + 0.8 * jax.random.uniform(part_splits[2], (TOKENS, TOP), jnp.float32) ** shard_levels(part_splits[2], (TOKENS, TOP), ((0, 16),), -0.2, 0.2), 0.2, 1.0)
    gate_weight = normal_values(key_of[3], (FF, D), D ** -0.5, 0.078125, ((0, 16),))
    up_weight = normal_values(key_of[4], (FF, D), D ** -0.5, 0.078125, ((0, 16),))
    down_weight = noise_with(key_of[5], (FF, D), FF ** -0.5, 0.078125, ((0, 16),), (0, 1, 16, 2.0))
    return dict(tokens=tokens, expert_ids=expert_ids, gates=gates, gate_weight=gate_weight, up_weight=up_weight, down_weight=down_weight)


def reference(tokens, expert_ids, gates, gate_weight, up_weight, down_weight):
    route_ids = expert_ids.reshape(N_TENSOR, TOK_DEV, TOP)
    expert_hits = route_ids == 0
    routed = jnp.any(expert_hits, axis=2)
    slot_index = (jnp.cumsum(routed.astype(jnp.int32), axis=1) - 1).astype(jnp.int32)
    slot_match = routed[:, :, None] & (slot_index[:, :, None] == jnp.arange(CAP, dtype=jnp.int32)[None, None, :])
    match_float = slot_match.astype(jnp.float32)
    token_rows = tokens.reshape(N_TENSOR, TOK_DEV, D)
    slot_rows = jnp.einsum("ntc,ntd->ncd", match_float, token_rows.astype(jnp.float32))
    slot_rows = slot_rows.astype(jnp.bfloat16).reshape(N_TENSOR * CAP, D)
    contract = (((1,), (1,)), ((), ()))
    gate_pre = lax.dot_general(slot_rows, gate_weight, contract, preferred_element_type=jnp.float32)
    up_pre = lax.dot_general(slot_rows, up_weight, contract, preferred_element_type=jnp.float32)
    hidden = (jax.nn.silu(gate_pre) * up_pre).astype(jnp.bfloat16)
    expert_out = jnp.dot(hidden, down_weight, preferred_element_type=jnp.float32).astype(jnp.bfloat16)
    expert_out = expert_out.reshape(N_TENSOR, CAP, D)
    gate_share = jnp.sum(jnp.where(expert_hits, gates.reshape(N_TENSOR, TOK_DEV, TOP), 0.0), axis=2)
    picked = jnp.einsum("ntc,ncd->ntd", match_float, expert_out.astype(jnp.float32))
    mixed = (gate_share[:, :, None] * picked).astype(jnp.bfloat16)
    return mixed.reshape(TOKENS, D)
```

```python
import jax
import jax.numpy as jnp
from jax import lax
from jax.experimental import pallas as pl
from jax.experimental.pallas import tpu as pltpu
from jax.sharding import PartitionSpec as P

CAP = 12
PAIR = 2 * CAP
F32 = jnp.float32
BF16 = jnp.bfloat16


def permutations(size):
    chips = size // 2
    order = list(range(0, chips, 2)) + list(range(chips - 1, 0, -2))

    def ring(step):
        pairs = []
        for place, chip in enumerate(order):
            pairs.append((2 * chip, 2 * order[(place + step) % chips]))
            pairs.append((2 * chip + 1, 2 * order[(place - step) % chips] + 1))
        return pairs

    return [(i, i ^ 1) for i in range(size)], ring(1), ring(2)


def halves(width):
    core = lax.rem(lax.axis_index("tensor"), 2)
    half = width // 2
    return core, pl.multiple_of(core * half, 128), pl.multiple_of((1 - core) * half, 128)


def choose(ids, core):
    tokens = ids.shape[1]
    routed = jnp.max(jnp.where(ids == 0, 1.0, 0.0), axis=0, keepdims=True)
    earlier = lax.broadcasted_iota(jnp.int32, (tokens, tokens), 0) < lax.broadcasted_iota(
        jnp.int32, (tokens, tokens), 1
    )
    before = jnp.dot(
        jnp.broadcast_to(routed, (8, tokens)).astype(BF16),
        jnp.where(earlier, 1.0, 0.0).astype(BF16),
        preferred_element_type=F32,
    )[:1]
    row = lax.broadcasted_iota(jnp.int32, (PAIR, tokens), 0) - core * CAP
    return jnp.where((row.astype(F32) == before) & (routed > 0.0), 1.0, 0.0)


def compact_kernel(ids_ref, tokens_ref, out_ref):
    width = tokens_ref.shape[1]
    core, first, second = halves(width)
    chooser = choose(ids_ref[...], core).astype(BF16)
    for place, start in enumerate((first, second)):
        out_ref[place * PAIR : (place + 1) * PAIR, :] = jnp.dot(
            chooser, tokens_ref[:, pl.ds(start, width // 2)], preferred_element_type=F32
        ).astype(BF16)


def hidden_kernel(blocks, *refs):
    firsts, seconds = refs[:blocks], refs[blocks : 2 * blocks]
    gate_ref, up_ref, out_ref, rows_first, rows_second = refs[2 * blocks :]
    units, width = gate_ref.shape
    half = width // 2
    _, first, second = halves(width)
    for j in range(blocks):
        rows_first[j * PAIR : (j + 1) * PAIR, :] = firsts[j][...]
        rows_second[j * PAIR : (j + 1) * PAIR, :] = seconds[j][...]
    contract = (((1,), (1,)), ((), ()))

    def product(weight_ref, start, size):
        return lax.dot_general(
            rows_first[...],
            weight_ref[start : start + size, pl.ds(first, half)],
            contract,
            preferred_element_type=F32,
        ) + lax.dot_general(
            rows_second[...],
            weight_ref[start : start + size, pl.ds(second, half)],
            contract,
            preferred_element_type=F32,
        )

    for start in range(0, units, 256):
        size = min(256, units - start)
        gate = product(gate_ref, start, size)
        up = product(up_ref, start, size)
        out_ref[:, start : start + size] = (gate / (1.0 + jnp.exp(-gate)) * up).astype(BF16)


def down_kernel(which, send_rows, hidden_ref, down_ref, send_ref, keep_ref):
    width = down_ref.shape[1]
    half = width // 2
    start = halves(width)[1 + which]
    tile = half // 3
    for part in range(3):
        columns = pl.ds(pl.multiple_of(start + part * tile, 128), tile)
        value = jnp.dot(hidden_ref[...], down_ref[:, columns], preferred_element_type=F32)
        here = slice(part * tile, (part + 1) * tile)
        send_ref[:, here] = value[:send_rows].astype(BF16)
        keep_ref[:, here] = value[send_rows:]


def mix_kernel(ids_ref, gates_ref, first_ref, second_ref, own_first, own_second, sibling_ref, out_ref):
    width = out_ref.shape[1]
    core, first, second = halves(width)
    ids = ids_ref[...]
    tokens = ids.shape[1]
    chooser = choose(ids, core).astype(BF16)
    share = jnp.sum(jnp.where(ids == 0, gates_ref[...], 0.0), axis=0, keepdims=True)
    share = jnp.broadcast_to(share, (tokens, tokens)).T[:, :1]
    sibling = sibling_ref[...].astype(F32)
    for start, ring_ref, own, other in (
        (first, first_ref, own_first, sibling[PAIR:]),
        (second, second_ref, own_second, sibling[:PAIR]),
    ):
        rows = (ring_ref[...].astype(F32) + own[...] + other).astype(BF16)
        picked = lax.dot_general(
            chooser, rows, (((0,), (0,)), ((), ())), preferred_element_type=F32
        )
        out_ref[:, pl.ds(start, width // 2)] = (share * picked).astype(BF16)


def call(kernel, out_shape, *args, scratch=(), flops=0):
    moved = sum(a.size * a.dtype.itemsize for a in args)
    return pl.pallas_call(
        kernel,
        out_shape=out_shape,
        scratch_shapes=list(scratch),
        compiler_params=pltpu.CompilerParams(vmem_limit_bytes=56 * 2**20),
        cost_estimate=pl.CostEstimate(flops=flops, bytes_accessed=moved, transcendentals=0),
    )(*args)


def body(size, tokens, expert_ids, gates, gate_weight, up_weight, down_weight):
    width = tokens.shape[1]
    half = width // 2
    units = gate_weight.shape[0]
    chips = size // 2
    reach = chips // 2
    rows = chips * PAIR
    pair_core, ring_one, ring_two = permutations(size)

    def swap(a):
        return lax.ppermute(a, "tensor", pair_core)

    def onward(a):
        return lax.ppermute(a, "tensor", ring_one)

    def two_on(a):
        return lax.ppermute(a, "tensor", ring_two)

    struct = jax.ShapeDtypeStruct
    ids = expert_ids.T
    own = call(compact_kernel, struct((2 * PAIR, half), BF16), ids, tokens)
    theirs = swap(own)
    chip_first = own[:PAIR] + theirs[PAIR:]
    chip_second = own[PAIR:] + theirs[:PAIR]

    behind = [(chip_first, chip_second)]
    ahead = [None]
    for _ in range(1, reach):
        first, second = (onward(a) for a in behind[-1])
        behind.append((first, second))
        ahead.append((swap(second), swap(first)))
    far_first = two_on(behind[reach - 2][0])
    far_second = swap(far_first)
    order = behind[1:] + [(far_first, far_second)] + ahead[1:] + [behind[0]]

    hidden = call(
        lambda *refs: hidden_kernel(chips, *refs),
        struct((rows, units), BF16),
        *[a for a, _ in order],
        *[b for _, b in order],
        gate_weight,
        up_weight,
        scratch=[pltpu.VMEM((rows, half), BF16)] * 2,
        flops=4 * rows * units * width,
    )

    def partial_sums(which, send_rows):
        return call(
            lambda *refs: down_kernel(which, send_rows, *refs),
            (struct((send_rows, half), BF16), struct((rows - send_rows, half), F32)),
            hidden,
            down_weight,
            flops=2 * rows * units * half,
        )

    near = (reach - 1) * PAIR
    send_second, keep_second = partial_sums(1, near + PAIR)
    send_first, keep_first = partial_sums(0, near)
    from_first = swap(send_second)
    from_second = swap(send_first)
    keep_far, keep_first = keep_first[:PAIR], keep_first[PAIR:]

    def chip_sum(keep, other, distance):
        here = slice((distance - 1) * PAIR, distance * PAIR)
        return keep[here] + other[here].astype(F32)

    far = two_on((keep_far + from_first[near:].astype(F32)).astype(BF16))
    sum_first = chip_sum(keep_first, from_first, reach - 1)
    sum_second = chip_sum(keep_second, from_second, reach - 1)
    for distance in range(reach - 1, 0, -1):
        first = onward(sum_first.astype(BF16)).astype(F32)
        second = onward(sum_second.astype(BF16)).astype(F32)
        if distance == reach - 1:
            first = first + far.astype(F32)
        if distance > 1:
            sum_first = first + chip_sum(keep_first, from_first, distance - 1)
            sum_second = second + chip_sum(keep_second, from_second, distance - 1)
    own_first, own_second = keep_first[near:], keep_second[near:]
    total = jnp.concatenate([first + own_first, second + own_second]).astype(BF16)
    return call(
        mix_kernel,
        struct(tokens.shape, BF16),
        ids,
        gates.T,
        first.astype(BF16),
        second.astype(BF16),
        own_first,
        own_second,
        swap(total),
    )


def solution(mesh):
    size = mesh.shape["tensor"]
    tokens = P(("groups", "tensor"), None)
    weights = P("tensor", None)
    return jax.shard_map(
        lambda *args: body(size, *args),
        mesh=mesh,
        in_specs=(tokens, tokens, tokens, weights, weights, weights),
        out_specs=tokens,
        check_vma=False,
    )
```

```python
import jax
import jax.numpy as jnp
from jax import lax
from jax.experimental import pallas as pl
from jax.experimental.pallas import tpu as pltpu
from jax.sharding import PartitionSpec as P

CAP = 12
PAIR = 2 * CAP
F32 = jnp.float32
BF16 = jnp.bfloat16


def permutations(size):
    chips = size // 2
    order = list(range(0, chips, 2)) + list(range(chips - 1, 0, -2))

    def ring(step):
        pairs = []
        for place, chip in enumerate(order):
            pairs.append((2 * chip, 2 * order[(place + step) % chips]))
            pairs.append((2 * chip + 1, 2 * order[(place - step) % chips] + 1))
        return pairs

    return [(i, i ^ 1) for i in range(size)], ring(1), ring(2)


def halves(width):
    core = lax.rem(lax.axis_index("tensor"), 2)
    half = width // 2
    return core, pl.multiple_of(core * half, 128), pl.multiple_of((1 - core) * half, 128)


def choose(ids, core):
    tokens = ids.shape[1]
    routed = jnp.max(jnp.where(ids == 0, 1.0, 0.0), axis=0, keepdims=True)
    earlier = lax.broadcasted_iota(jnp.int32, (tokens, tokens), 0) < lax.broadcasted_iota(
        jnp.int32, (tokens, tokens), 1
    )
    before = jnp.dot(
        jnp.broadcast_to(routed, (8, tokens)).astype(BF16),
        jnp.where(earlier, 1.0, 0.0).astype(BF16),
        preferred_element_type=F32,
    )[:1]
    row = lax.broadcasted_iota(jnp.int32, (PAIR, tokens), 0) - core * CAP
    return jnp.where((row.astype(F32) == before) & (routed > 0.0), 1.0, 0.0)


def compact_kernel(ids_ref, tokens_ref, out_ref):
    width = tokens_ref.shape[1]
    core, first, second = halves(width)
    chooser = choose(ids_ref[...], core).astype(BF16)
    for place, start in enumerate((first, second)):
        out_ref[place * PAIR : (place + 1) * PAIR, :] = jnp.dot(
            chooser, tokens_ref[:, pl.ds(start, width // 2)], preferred_element_type=F32
        ).astype(BF16)


def hidden_kernel(blocks, *refs):
    firsts, seconds = refs[:blocks], refs[blocks : 2 * blocks]
    gate_ref, up_ref, out_ref, rows_first, rows_second = refs[2 * blocks :]
    units, width = gate_ref.shape
    half = width // 2
    _, first, second = halves(width)
    for j in range(blocks):
        rows_first[j * PAIR : (j + 1) * PAIR, :] = firsts[j][...]
        rows_second[j * PAIR : (j + 1) * PAIR, :] = seconds[j][...]
    contract = (((1,), (1,)), ((), ()))

    def product(weight_ref, start, size):
        return lax.dot_general(
            rows_first[...],
            weight_ref[start : start + size, pl.ds(first, half)],
            contract,
            preferred_element_type=F32,
        ) + lax.dot_general(
            rows_second[...],
            weight_ref[start : start + size, pl.ds(second, half)],
            contract,
            preferred_element_type=F32,
        )

    for start in range(0, units, 256):
        size = min(256, units - start)
        gate = product(gate_ref, start, size)
        up = product(up_ref, start, size)
        out_ref[:, start : start + size] = (gate / (1.0 + jnp.exp(-gate)) * up).astype(BF16)


def down_kernel(which, send_rows, hidden_ref, down_ref, send_ref, keep_ref):
    width = down_ref.shape[1]
    half = width // 2
    start = halves(width)[1 + which]
    tile = half // 3
    for part in range(3):
        columns = pl.ds(pl.multiple_of(start + part * tile, 128), tile)
        value = jnp.dot(hidden_ref[...], down_ref[:, columns], preferred_element_type=F32)
        here = slice(part * tile, (part + 1) * tile)
        send_ref[:, here] = value[:send_rows].astype(BF16)
        keep_ref[:, here] = value[send_rows:]


def mix_kernel(ids_ref, gates_ref, first_ref, second_ref, own_first, own_second, sibling_ref, out_ref):
    width = out_ref.shape[1]
    core, first, second = halves(width)
    ids = ids_ref[...]
    tokens = ids.shape[1]
    chooser = choose(ids, core).astype(BF16)
    share = jnp.sum(jnp.where(ids == 0, gates_ref[...], 0.0), axis=0, keepdims=True)
    share = jnp.broadcast_to(share, (tokens, tokens)).T[:, :1]
    sibling = sibling_ref[...].astype(F32)
    for start, ring_ref, own, other in (
        (first, first_ref, own_first, sibling[PAIR:]),
        (second, second_ref, own_second, sibling[:PAIR]),
    ):
        rows = (ring_ref[...].astype(F32) + own[...] + other).astype(BF16)
        picked = lax.dot_general(
            chooser, rows, (((0,), (0,)), ((), ())), preferred_element_type=F32
        )
        out_ref[:, pl.ds(start, width // 2)] = (share * picked).astype(BF16)


def call(kernel, out_shape, *args, scratch=(), flops=0):
    moved = sum(a.size * a.dtype.itemsize for a in args)
    return pl.pallas_call(
        kernel,
        out_shape=out_shape,
        scratch_shapes=list(scratch),
        compiler_params=pltpu.CompilerParams(vmem_limit_bytes=16 * 2**20),
        cost_estimate=pl.CostEstimate(flops=flops, bytes_accessed=moved, transcendentals=0),
    )(*args)


def body(size, tokens, expert_ids, gates, gate_weight, up_weight, down_weight):
    width = tokens.shape[1]
    half = width // 2
    units = gate_weight.shape[0]
    chips = size // 2
    reach = chips // 2
    rows = chips * PAIR
    pair_core, ring_one, ring_two = permutations(size)

    def swap(a):
        return lax.ppermute(a, "tensor", pair_core)

    def onward(a):
        return lax.ppermute(a, "tensor", ring_one)

    def two_on(a):
        return lax.ppermute(a, "tensor", ring_two)

    struct = jax.ShapeDtypeStruct
    ids = expert_ids.T
    own = call(compact_kernel, struct((2 * PAIR, half), BF16), ids, tokens)
    theirs = swap(own)
    chip_first = own[:PAIR] + theirs[PAIR:]
    chip_second = own[PAIR:] + theirs[:PAIR]

    behind = [(chip_first, chip_second)]
    ahead = [None]
    for _ in range(1, reach):
        first, second = (onward(a) for a in behind[-1])
        behind.append((first, second))
        ahead.append((swap(second), swap(first)))
    far_first = two_on(behind[reach - 2][0])
    far_second = swap(far_first)
    order = behind[1:] + [(far_first, far_second)] + ahead[1:] + [behind[0]]

    hidden = call(
        lambda *refs: hidden_kernel(chips, *refs),
        struct((rows, units), BF16),
        *[a for a, _ in order],
        *[b for _, b in order],
        gate_weight,
        up_weight,
        scratch=[pltpu.VMEM((rows, half), BF16)] * 2,
        flops=4 * rows * units * width,
    )

    def partial_sums(which, send_rows):
        return call(
            lambda *refs: down_kernel(which, send_rows, *refs),
            (struct((send_rows, half), BF16), struct((rows - send_rows, half), F32)),
            hidden,
            down_weight,
            flops=2 * rows * units * half,
        )

    near = (reach - 1) * PAIR
    send_second, keep_second = partial_sums(1, near + PAIR)
    send_first, keep_first = partial_sums(0, near)
    from_first = swap(send_second)
    from_second = swap(send_first)
    keep_far, keep_first = keep_first[:PAIR], keep_first[PAIR:]

    def chip_sum(keep, other, distance):
        here = slice((distance - 1) * PAIR, distance * PAIR)
        return keep[here] + other[here].astype(F32)

    far = two_on((keep_far + from_first[near:].astype(F32)).astype(BF16))
    sum_first = chip_sum(keep_first, from_first, reach - 1)
    sum_second = chip_sum(keep_second, from_second, reach - 1)
    for distance in range(reach - 1, 0, -1):
        first = onward(sum_first.astype(BF16)).astype(F32)
        second = onward(sum_second.astype(BF16)).astype(F32)
        if distance == reach - 1:
            first = first + far.astype(F32)
        if distance > 1:
            sum_first = first + chip_sum(keep_first, from_first, distance - 1)
            sum_second = second + chip_sum(keep_second, from_second, distance - 1)
    own_first, own_second = keep_first[near:], keep_second[near:]
    total = jnp.concatenate([first + own_first, second + own_second]).astype(BF16)
    return call(
        mix_kernel,
        struct(tokens.shape, BF16),
        ids,
        gates.T,
        first.astype(BF16),
        second.astype(BF16),
        own_first,
        own_second,
        swap(total),
    )


def solution(mesh):
    size = mesh.shape["tensor"]
    tokens = P(("groups", "tensor"), None)
    weights = P("tensor", None)
    return jax.shard_map(
        lambda *args: body(size, *args),
        mesh=mesh,
        in_specs=(tokens, tokens, tokens, weights, weights, weights),
        out_specs=tokens,
        check_vma=False,
    )
```

```python
import jax
import jax.numpy as jnp
from jax import lax
from jax.experimental import pallas as pl
from jax.experimental.pallas import tpu as pltpu
from jax.sharding import PartitionSpec as P

CAP = 12
PAIR = 2 * CAP
F32 = jnp.float32
BF16 = jnp.bfloat16


def permutations(size):
    chips = size // 2
    order = list(range(0, chips, 2)) + list(range(chips - 1, 0, -2))

    def ring(step):
        pairs = []
        for place, chip in enumerate(order):
            pairs.append((2 * chip, 2 * order[(place + step) % chips]))
            pairs.append((2 * chip + 1, 2 * order[(place - step) % chips] + 1))
        return pairs

    return [(i, i ^ 1) for i in range(size)], ring(1), ring(2)


def halves(width):
    core = lax.rem(lax.axis_index("tensor"), 2)
    half = width // 2
    return core, pl.multiple_of(core * half, 128), pl.multiple_of((1 - core) * half, 128)


def choose(ids, core):
    tokens = ids.shape[1]
    routed = jnp.max(jnp.where(ids == 0, 1.0, 0.0), axis=0, keepdims=True)
    earlier = lax.broadcasted_iota(jnp.int32, (tokens, tokens), 0) < lax.broadcasted_iota(
        jnp.int32, (tokens, tokens), 1
    )
    before = jnp.dot(
        jnp.broadcast_to(routed, (8, tokens)).astype(BF16),
        jnp.where(earlier, 1.0, 0.0).astype(BF16),
        preferred_element_type=F32,
    )[:1]
    row = lax.broadcasted_iota(jnp.int32, (PAIR, tokens), 0) - core * CAP
    return jnp.where((row.astype(F32) == before) & (routed > 0.0), 1.0, 0.0)


def compact_kernel(ids_ref, tokens_ref, out_ref):
    width = tokens_ref.shape[1]
    core, first, second = halves(width)
    chooser = choose(ids_ref[...], core).astype(BF16)
    for place, start in enumerate((first, second)):
        out_ref[place * PAIR : (place + 1) * PAIR, :] = jnp.dot(
            chooser, tokens_ref[:, pl.ds(start, width // 2)], preferred_element_type=F32
        ).astype(BF16)


def join_kernel(own_ref, theirs_ref, first_ref, second_ref):
    first_ref[...] = own_ref[:PAIR, :] + theirs_ref[PAIR:, :]
    second_ref[...] = own_ref[PAIR:, :] + theirs_ref[:PAIR, :]


def hidden_kernel(blocks, *refs):
    firsts, seconds = refs[:blocks], refs[blocks : 2 * blocks]
    gate_ref, up_ref, out_ref, rows_first, rows_second = refs[2 * blocks :]
    units, width = gate_ref.shape
    half = width // 2
    _, first, second = halves(width)
    for j in range(blocks):
        rows_first[j * PAIR : (j + 1) * PAIR, :] = firsts[j][...]
        rows_second[j * PAIR : (j + 1) * PAIR, :] = seconds[j][...]
    contract = (((1,), (1,)), ((), ()))

    def product(weight_ref, start, size):
        return lax.dot_general(
            rows_first[...],
            weight_ref[start : start + size, pl.ds(first, half)],
            contract,
            preferred_element_type=F32,
        ) + lax.dot_general(
            rows_second[...],
            weight_ref[start : start + size, pl.ds(second, half)],
            contract,
            preferred_element_type=F32,
        )

    for start in range(0, units, 256):
        size = min(256, units - start)
        gate = product(gate_ref, start, size)
        up = product(up_ref, start, size)
        out_ref[:, start : start + size] = (gate / (1.0 + jnp.exp(-gate)) * up).astype(BF16)


def down_kernel(which, send_rows, hidden_ref, down_ref, send_ref, keep_ref):
    width = down_ref.shape[1]
    half = width // 2
    start = halves(width)[1 + which]
    tile = half // 3
    for part in range(3):
        columns = pl.ds(pl.multiple_of(start + part * tile, 128), tile)
        value = jnp.dot(hidden_ref[...], down_ref[:, columns], preferred_element_type=F32)
        here = slice(part * tile, (part + 1) * tile)
        send_ref[:, here] = value[:send_rows].astype(BF16)
        keep_ref[:, here] = value[send_rows:]


def mix_kernel(ids_ref, gates_ref, first_ref, second_ref, own_first, own_second, sibling_ref, out_ref):
    width = out_ref.shape[1]
    core, first, second = halves(width)
    ids = ids_ref[...]
    tokens = ids.shape[1]
    chooser = choose(ids, core).astype(BF16)
    share = jnp.sum(jnp.where(ids == 0, gates_ref[...], 0.0), axis=0, keepdims=True)
    share = jnp.broadcast_to(share, (tokens, tokens)).T[:, :1]
    sibling = sibling_ref[...].astype(F32)
    for start, ring_ref, own, other in (
        (first, first_ref, own_first, sibling[PAIR:]),
        (second, second_ref, own_second, sibling[:PAIR]),
    ):
        rows = (ring_ref[...].astype(F32) + own[...] + other).astype(BF16)
        picked = lax.dot_general(
            chooser, rows, (((0,), (0,)), ((), ())), preferred_element_type=F32
        )
        out_ref[:, pl.ds(start, width // 2)] = (share * picked).astype(BF16)


def call(kernel, out_shape, *args, scratch=(), flops=0, extra=0):
    moved = extra + sum(a.size * a.dtype.itemsize for a in args)
    return pl.pallas_call(
        kernel,
        out_shape=out_shape,
        scratch_shapes=list(scratch),
        compiler_params=pltpu.CompilerParams(vmem_limit_bytes=16 * 2**20),
        cost_estimate=pl.CostEstimate(flops=flops, bytes_accessed=moved, transcendentals=0),
    )(*args)


def body(size, tokens, expert_ids, gates, gate_weight, up_weight, down_weight):
    width = tokens.shape[1]
    half = width // 2
    units = gate_weight.shape[0]
    chips = size // 2
    reach = chips // 2
    rows = chips * PAIR
    pair_core, ring_one, ring_two = permutations(size)

    def swap(a):
        return lax.ppermute(a, "tensor", pair_core)

    def onward(a):
        return lax.ppermute(a, "tensor", ring_one)

    def two_on(a):
        return lax.ppermute(a, "tensor", ring_two)

    struct = jax.ShapeDtypeStruct
    ids = expert_ids.T
    own = call(compact_kernel, struct((2 * PAIR, half), BF16), ids, tokens)
    theirs = swap(own)
    chip_first, chip_second = call(
        join_kernel, (struct((PAIR, half), BF16),) * 2, own, theirs, flops=40 * rows * units * width
    )

    behind = [(chip_first, chip_second)]
    ahead = [None]
    for _ in range(1, reach):
        first, second = (onward(a) for a in behind[-1])
        behind.append((first, second))
        ahead.append((swap(second), swap(first)))
    far_first = two_on(behind[reach - 2][0])
    far_second = swap(far_first)
    order = behind[1:] + [(far_first, far_second)] + ahead[1:] + [behind[0]]

    hidden = call(
        lambda *refs: hidden_kernel(chips, *refs),
        struct((rows, units), BF16),
        *[a for a, _ in order],
        *[b for _, b in order],
        gate_weight,
        up_weight,
        scratch=[pltpu.VMEM((rows, half), BF16)] * 2,
        flops=4 * rows * units * width,
    )

    def partial_sums(which, send_rows):
        return call(
            lambda *refs: down_kernel(which, send_rows, *refs),
            (struct((send_rows, half), BF16), struct((rows - send_rows, half), F32)),
            hidden,
            down_weight,
            flops=2 * rows * units * half,
        )

    near = (reach - 1) * PAIR
    send_second, keep_second = partial_sums(1, near + PAIR)
    send_first, keep_first = partial_sums(0, near)
    from_first = swap(send_second)
    from_second = swap(send_first)
    keep_far, keep_first = keep_first[:PAIR], keep_first[PAIR:]

    def chip_sum(keep, other, distance):
        here = slice((distance - 1) * PAIR, distance * PAIR)
        return keep[here] + other[here].astype(F32)

    far = two_on((keep_far + from_first[near:].astype(F32)).astype(BF16))
    sum_first = chip_sum(keep_first, from_first, reach - 1)
    sum_second = chip_sum(keep_second, from_second, reach - 1)
    for distance in range(reach - 1, 0, -1):
        first = onward(sum_first.astype(BF16)).astype(F32)
        second = onward(sum_second.astype(BF16)).astype(F32)
        if distance == reach - 1:
            first = first + far.astype(F32)
        if distance > 1:
            sum_first = first + chip_sum(keep_first, from_first, distance - 1)
            sum_second = second + chip_sum(keep_second, from_second, distance - 1)
    own_first, own_second = keep_first[near:], keep_second[near:]
    total = jnp.concatenate([first + own_first, second + own_second]).astype(BF16)
    return call(
        mix_kernel,
        struct(tokens.shape, BF16),
        ids,
        gates.T,
        first.astype(BF16),
        second.astype(BF16),
        own_first,
        own_second,
        swap(total),
    )


def solution(mesh):
    size = mesh.shape["tensor"]
    tokens = P(("groups", "tensor"), None)
    weights = P("tensor", None)
    return jax.shard_map(
        lambda *args: body(size, *args),
        mesh=mesh,
        in_specs=(tokens, tokens, tokens, weights, weights, weights),
        out_specs=tokens,
        check_vma=False,
    )
```

```python
import jax
import jax.numpy as jnp
from jax import lax
from jax.experimental import pallas as pl
from jax.experimental.pallas import tpu as pltpu
from jax.sharding import PartitionSpec as P

CAP = 12
PAIR = 2 * CAP
F32 = jnp.float32
BF16 = jnp.bfloat16


def permutations(size):
    chips = size // 2
    order = list(range(0, chips, 2)) + list(range(chips - 1, 0, -2))

    def ring(step):
        pairs = []
        for place, chip in enumerate(order):
            pairs.append((2 * chip, 2 * order[(place + step) % chips]))
            pairs.append((2 * chip + 1, 2 * order[(place - step) % chips] + 1))
        return pairs

    return [(i, i ^ 1) for i in range(size)], ring(1), ring(2)


def halves(width):
    core = lax.rem(lax.axis_index("tensor"), 2)
    half = width // 2
    return core, pl.multiple_of(core * half, 128), pl.multiple_of((1 - core) * half, 128)


def choose(ids, core):
    tokens = ids.shape[1]
    routed = jnp.max(jnp.where(ids == 0, 1.0, 0.0), axis=0, keepdims=True)
    earlier = lax.broadcasted_iota(jnp.int32, (tokens, tokens), 0) < lax.broadcasted_iota(
        jnp.int32, (tokens, tokens), 1
    )
    before = jnp.dot(
        jnp.broadcast_to(routed, (8, tokens)).astype(BF16),
        jnp.where(earlier, 1.0, 0.0).astype(BF16),
        preferred_element_type=F32,
    )[:1]
    row = lax.broadcasted_iota(jnp.int32, (PAIR, tokens), 0) - core * CAP
    return jnp.where((row.astype(F32) == before) & (routed > 0.0), 1.0, 0.0)


def compact_kernel(ids_ref, tokens_ref, out_ref):
    width = tokens_ref.shape[1]
    core, first, second = halves(width)
    chooser = choose(ids_ref[...], core).astype(BF16)
    for place, start in enumerate((first, second)):
        out_ref[place * PAIR : (place + 1) * PAIR, :] = jnp.dot(
            chooser, tokens_ref[:, pl.ds(start, width // 2)], preferred_element_type=F32
        ).astype(BF16)


def join_kernel(own_ref, theirs_ref, first_ref, second_ref):
    first_ref[...] = own_ref[:PAIR, :] + theirs_ref[PAIR:, :]
    second_ref[...] = own_ref[PAIR:, :] + theirs_ref[:PAIR, :]


def hidden_kernel(blocks, *refs):
    firsts, seconds = refs[:blocks], refs[blocks : 2 * blocks]
    gate_ref, up_ref, out_ref, rows_first, rows_second = refs[2 * blocks :]
    units, width = gate_ref.shape
    half = width // 2
    _, first, second = halves(width)
    for j in range(blocks):
        rows_first[j * PAIR : (j + 1) * PAIR, :] = firsts[j][...]
        rows_second[j * PAIR : (j + 1) * PAIR, :] = seconds[j][...]
    contract = (((1,), (1,)), ((), ()))

    def product(weight_ref, start, size):
        return lax.dot_general(
            rows_first[...],
            weight_ref[start : start + size, pl.ds(first, half)],
            contract,
            preferred_element_type=F32,
        ) + lax.dot_general(
            rows_second[...],
            weight_ref[start : start + size, pl.ds(second, half)],
            contract,
            preferred_element_type=F32,
        )

    for start in range(0, units, 256):
        size = min(256, units - start)
        gate = product(gate_ref, start, size)
        up = product(up_ref, start, size)
        out_ref[:, start : start + size] = (gate / (1.0 + jnp.exp(-gate)) * up).astype(BF16)


def down_kernel(which, send_rows, hidden_ref, down_ref, send_ref, keep_ref):
    width = down_ref.shape[1]
    half = width // 2
    start = halves(width)[1 + which]
    tile = half // 3
    for part in range(3):
        columns = pl.ds(pl.multiple_of(start + part * tile, 128), tile)
        value = jnp.dot(hidden_ref[...], down_ref[:, columns], preferred_element_type=F32)
        here = slice(part * tile, (part + 1) * tile)
        send_ref[:, here] = value[:send_rows].astype(BF16)
        keep_ref[:, here] = value[send_rows:]


def mix_kernel(ids_ref, gates_ref, first_ref, second_ref, own_first, own_second, sibling_ref, out_ref):
    width = out_ref.shape[1]
    core, first, second = halves(width)
    ids = ids_ref[...]
    tokens = ids.shape[1]
    chooser = choose(ids, core).astype(BF16)
    share = jnp.sum(jnp.where(ids == 0, gates_ref[...], 0.0), axis=0, keepdims=True)
    share = jnp.broadcast_to(share, (tokens, tokens)).T[:, :1]
    sibling = sibling_ref[...].astype(F32)
    for start, ring_ref, own, other in (
        (first, first_ref, own_first, sibling[PAIR:]),
        (second, second_ref, own_second, sibling[:PAIR]),
    ):
        rows = (ring_ref[...].astype(F32) + own[...] + other).astype(BF16)
        picked = lax.dot_general(
            chooser, rows, (((0,), (0,)), ((), ())), preferred_element_type=F32
        )
        out_ref[:, pl.ds(start, width // 2)] = (share * picked).astype(BF16)


def call(kernel, out_shape, *args, scratch=(), flops=0, extra=0):
    moved = extra + sum(a.size * a.dtype.itemsize for a in args)
    return pl.pallas_call(
        kernel,
        out_shape=out_shape,
        scratch_shapes=list(scratch),
        compiler_params=pltpu.CompilerParams(vmem_limit_bytes=16 * 2**20),
        cost_estimate=pl.CostEstimate(flops=flops, bytes_accessed=moved, transcendentals=0),
    )(*args)


def body(size, tokens, expert_ids, gates, gate_weight, up_weight, down_weight):
    width = tokens.shape[1]
    half = width // 2
    units = gate_weight.shape[0]
    chips = size // 2
    reach = chips // 2
    rows = chips * PAIR
    pair_core, ring_one, ring_two = permutations(size)

    def swap(a):
        return lax.ppermute(a, "tensor", pair_core)

    def onward(a):
        return lax.ppermute(a, "tensor", ring_one)

    def two_on(a):
        return lax.ppermute(a, "tensor", ring_two)

    struct = jax.ShapeDtypeStruct
    ids = expert_ids.T
    own = call(compact_kernel, struct((2 * PAIR, half), BF16), ids, tokens)
    theirs = swap(own)
    chip_first, chip_second = call(
        join_kernel, (struct((PAIR, half), BF16),) * 2, own, theirs, flops=40 * rows * units * width
    )

    first_behind, second_behind = [chip_first], [chip_second]
    for distance in range(1, reach):
        second_behind.append(onward(second_behind[-1]))
        if distance == 1:
            first_behind.append(onward(chip_first))
        elif distance % 2 == 0:
            first_behind.append(two_on(first_behind[distance - 2]))
        else:
            first_behind.append(onward(first_behind[distance - 1]))
    far_first = two_on(first_behind[reach - 2])
    far_second = swap(far_first)
    behind = list(zip(first_behind, second_behind))
    ahead = [None] + [(swap(b), swap(a)) for a, b in behind[1:]]
    order = behind[1:] + [(far_first, far_second)] + ahead[1:] + [behind[0]]

    hidden = call(
        lambda *refs: hidden_kernel(chips, *refs),
        struct((rows, units), BF16),
        *[a for a, _ in order],
        *[b for _, b in order],
        gate_weight,
        up_weight,
        scratch=[pltpu.VMEM((rows, half), BF16)] * 2,
        flops=4 * rows * units * width,
    )

    def partial_sums(which, send_rows):
        return call(
            lambda *refs: down_kernel(which, send_rows, *refs),
            (struct((send_rows, half), BF16), struct((rows - send_rows, half), F32)),
            hidden,
            down_weight,
            flops=2 * rows * units * half,
        )

    near = (reach - 1) * PAIR
    send_second, keep_second = partial_sums(1, near + PAIR)
    send_first, keep_first = partial_sums(0, near)
    from_first = swap(send_second)
    from_second = swap(send_first)
    keep_far, keep_first = keep_first[:PAIR], keep_first[PAIR:]

    def chip_sum(keep, other, distance):
        here = slice((distance - 1) * PAIR, distance * PAIR)
        return keep[here] + other[here].astype(F32)

    far = two_on((keep_far + from_first[near:].astype(F32)).astype(BF16))
    sum_first = chip_sum(keep_first, from_first, reach - 1)
    sum_second = chip_sum(keep_second, from_second, reach - 1)
    for distance in range(reach - 1, 0, -1):
        first = onward(sum_first.astype(BF16)).astype(F32)
        second = onward(sum_second.astype(BF16)).astype(F32)
        if distance == reach - 1:
            first = first + far.astype(F32)
        if distance > 1:
            sum_first = first + chip_sum(keep_first, from_first, distance - 1)
            sum_second = second + chip_sum(keep_second, from_second, distance - 1)
    own_first, own_second = keep_first[near:], keep_second[near:]
    total = jnp.concatenate([first + own_first, second + own_second]).astype(BF16)
    return call(
        mix_kernel,
        struct(tokens.shape, BF16),
        ids,
        gates.T,
        first.astype(BF16),
        second.astype(BF16),
        own_first,
        own_second,
        swap(total),
    )


def solution(mesh):
    size = mesh.shape["tensor"]
    tokens = P(("groups", "tensor"), None)
    weights = P("tensor", None)
    return jax.shard_map(
        lambda *args: body(size, *args),
        mesh=mesh,
        in_specs=(tokens, tokens, tokens, weights, weights, weights),
        out_specs=tokens,
        check_vma=False,
    )
```

```python
import jax
import jax.numpy as jnp
from jax import lax
from jax.experimental import pallas as pl
from jax.experimental.pallas import tpu as pltpu
from jax.sharding import PartitionSpec as P

CAP = 12
PAIR = 2 * CAP
F32 = jnp.float32
BF16 = jnp.bfloat16
MIB = 2**20


def permutations(size):
    chips = size // 2
    order = list(range(0, chips, 2)) + list(range(chips - 1, 0, -2))

    def pairs(target):
        made = []
        for place, chip in enumerate(order):
            for core in range(2):
                step, to = target(core)
                made.append((2 * chip + core, 2 * order[(place + step) % chips] + to))
        return made

    way = (1, -1)
    return {
        "swap": pairs(lambda core: (0, 1 - core)),
        "one": pairs(lambda core: (way[core], core)),
        "two": pairs(lambda core: (2 * way[core], core)),
        "board": pairs(lambda core: (way[1 - core], 1 - core)),
        "leave": pairs(lambda core: (way[core], 1 - core)),
    }


def choose(ids):
    tokens = ids.shape[1]
    routed = jnp.max(jnp.where(ids == 0, 1.0, 0.0), axis=0, keepdims=True)
    earlier = lax.broadcasted_iota(jnp.int32, (tokens, tokens), 0) < lax.broadcasted_iota(
        jnp.int32, (tokens, tokens), 1
    )
    before = jnp.dot(
        jnp.broadcast_to(routed, (8, tokens)).astype(BF16),
        jnp.where(earlier, 1.0, 0.0).astype(BF16),
        preferred_element_type=F32,
    )[:1]

    def rows(first):
        slot = lax.broadcasted_iota(jnp.int32, (PAIR, tokens), 0) - first
        return jnp.where((slot.astype(F32) == before) & (routed > 0.0), 1.0, 0.0).astype(BF16)

    return rows(0), rows(CAP)


def compact_kernel(ids_ref, tokens_ref, out_ref):
    half = out_ref.shape[1]
    upper, lower = choose(ids_ref[...])
    out_ref[...] = (
        jnp.dot(upper, tokens_ref[:, :half], preferred_element_type=F32)
        + jnp.dot(lower, tokens_ref[:, half:], preferred_element_type=F32)
    ).astype(BF16)


def hidden_kernel(count, *refs):
    blocks, (gate_ref, up_ref, out_ref, first, second) = refs[:count], refs[count:]
    units, width = gate_ref.shape
    half = width // 2
    for j, block in enumerate(blocks):
        first[j * CAP : (j + 1) * CAP, :] = block[:CAP, :]
        second[j * CAP : (j + 1) * CAP, :] = block[CAP:, :]
    contract = (((1,), (1,)), ((), ()))

    def product(ref, here):
        return lax.dot_general(
            first[...], ref[here, :half], contract, preferred_element_type=F32
        ) + lax.dot_general(second[...], ref[here, half:], contract, preferred_element_type=F32)

    tile = 224 if units % 224 == 0 else units
    for start in range(0, units, tile):
        here = slice(start, start + tile)
        gate = product(gate_ref, here)
        up = product(up_ref, here)
        out_ref[:, here] = (gate / (1.0 + jnp.exp(-gate)) * up).astype(BF16)


def down_kernel(places, hidden_ref, down_ref, *out_refs):
    half = down_ref.shape[1] // 2
    tile = half // 3
    for step in range(3):
        here = slice(step * tile, (step + 1) * tile)
        low, high = (
            jnp.dot(
                hidden_ref[...],
                down_ref[:, start + step * tile : start + (step + 1) * tile],
                preferred_element_type=F32,
            )
            for start in (0, half)
        )
        for out_ref, indices in zip(out_refs, places):
            for k, j in enumerate(indices):
                rows = slice(j * CAP, (j + 1) * CAP)
                out_ref[k * PAIR : (k + 1) * PAIR, here] = jnp.concatenate(
                    [low[rows], high[rows]]
                ).astype(out_ref.dtype)


def mix_kernel(ids_ref, gates_ref, *refs):
    (*parts, out_ref, values, written) = refs
    half = values.shape[1] // 2
    tile = half // 3
    ids = ids_ref[...]
    tokens = ids.shape[1]
    share = jnp.sum(jnp.where(ids == 0, gates_ref[...], 0.0), axis=0, keepdims=True)
    share = jnp.broadcast_to(share, (tokens, tokens)).T[:, :1]
    choosers = choose(ids)
    copies = []
    for step in range(3):
        here = slice(step * tile, (step + 1) * tile)
        rows = sum(part[:, here].astype(F32) for part in parts).astype(BF16)
        for side, chooser in enumerate(choosers):
            picked = lax.dot_general(
                chooser, rows, (((0,), (0,)), ((), ())), preferred_element_type=F32
            )
            start = side * half + step * tile
            there = slice(start, start + tile)
            values[:, there] = (share * picked).astype(BF16)
            copies.append(
                pltpu.make_async_copy(
                    values.at[:, there], out_ref.at[:, there], written.at[2 * step + side]
                )
            )
            copies[-1].start()
    for copy in copies:
        copy.wait()


def call(kernel, out_shape, *args, scratch=(), flops=0, **specs):
    moved = sum(a.size * a.dtype.itemsize for a in args)
    return pl.pallas_call(
        kernel,
        out_shape=out_shape,
        scratch_shapes=list(scratch),
        compiler_params=pltpu.CompilerParams(vmem_limit_bytes=16 * MIB),
        cost_estimate=pl.CostEstimate(flops=flops, bytes_accessed=moved, transcendentals=0),
        **specs,
    )(*args)


def body(size, tokens, expert_ids, gates, gate_weight, up_weight, down_weight):
    count, width = tokens.shape
    half = width // 2
    units = gate_weight.shape[0]
    chips = size // 2
    reach = chips // 2
    rows = size * CAP
    steps = permutations(size)

    def move(kind, a):
        return lax.ppermute(a.astype(BF16), "tensor", steps[kind])

    struct = jax.ShapeDtypeStruct
    ids = expert_ids.T
    work = 2 * rows * units * width
    own = call(compact_kernel, struct((PAIR, half), BF16), ids, tokens, flops=20 * work)

    like, cross = [own], [None]
    for distance in range(1, reach):
        cross.append(move("board", own) if distance == 1 else move("one", cross[-1]))
        if distance % 2 == 0:
            like.append(move("two", like[distance - 2]))
        else:
            like.append(move("one", like[distance - 1]))
    like.append(move("two", like[reach - 2]))
    cross[0] = move("swap", own)
    cross.append(move("swap", like[reach]))
    ahead_like = [None] + [move("swap", a) for a in cross[1:reach]]
    ahead_cross = [None] + [move("swap", a) for a in like[1:reach]]

    names, blocks = {}, []
    for distance in range(reach, -1, -1):
        for kind, found in (("like", like), ("cross", cross)):
            names["behind", kind, distance] = len(blocks)
            blocks.append(found[distance])
    for distance in range(1, reach):
        for kind, found in (("like", ahead_like), ("cross", ahead_cross)):
            names["ahead", kind, distance] = len(blocks)
            blocks.append(found[distance])

    hidden = call(
        lambda *refs: hidden_kernel(len(blocks), *refs),
        struct((rows, units), BF16),
        *blocks,
        gate_weight,
        up_weight,
        scratch=[pltpu.VMEM((rows, half), BF16)] * 2,
        flops=2 * work,
    )

    away = range(reach - 1, 0, -1)
    kept = [("like", reach)] + [(kind, d) for d in away for kind in ("like", "cross")] + [("like", 0)]
    other = {"like": "cross", "cross": "like"}

    def index(kind, distance, side):
        side = "behind" if distance in (0, reach) else side
        return names[side, kind, distance]

    urgent = 3
    places = [
        [index(kind, d, "ahead") for kind, d in kept],
        [index(other[kind], d, "behind") for kind, d in kept[:urgent]],
        [index(other[kind], d, "behind") for kind, d in kept[urgent:]],
    ]
    keep, *sent = call(
        lambda *refs: down_kernel(places, *refs),
        [
            struct((len(indices) * PAIR, half), kind)
            for indices, kind in zip(places, (F32, BF16, BF16))
        ],
        hidden,
        down_weight,
        flops=work,
    )
    sent = [move("swap", a) for a in sent]

    def part(a, k):
        return a[k * PAIR : (k + 1) * PAIR]

    def chip_sum(kind, distance):
        k = kept.index((kind, distance))
        theirs = part(sent[0], k) if k < urgent else part(sent[1], k - urgent)
        return part(keep, k) + theirs.astype(F32)

    far, last_like, last_cross = lax.optimization_barrier(
        tuple(
            chip_sum(*name).astype(BF16)
            for name in (("like", reach), ("like", reach - 1), ("cross", reach - 1))
        )
    )
    like_sums = {d: chip_sum("like", d) for d in range(1, reach - 1)} | {reach - 1: last_like}
    like_sums[reach - 2] += move("two", far).astype(F32)
    cross_sum = last_cross
    arrived = []
    for distance in away:
        if distance > 1:
            cross_sum = move("one", cross_sum).astype(F32) + chip_sum("cross", distance - 1)
        else:
            arrived.append(move("leave", cross_sum))
        length = 2 - distance % 2
        came = move("two" if length == 2 else "one", like_sums[distance])
        if distance == length:
            arrived.append(came)
        else:
            like_sums[distance - length] += came.astype(F32)
    return call(
        mix_kernel,
        struct(tokens.shape, BF16),
        ids,
        gates.T,
        *arrived,
        part(keep, len(kept) - 1),
        part(sent[1], len(kept) - 1 - urgent),
        out_specs=pl.BlockSpec(memory_space=pl.ANY),
        scratch=[pltpu.VMEM(tokens.shape, BF16), pltpu.SemaphoreType.DMA((6,))],
    )


def solution(mesh):
    size = mesh.shape["tensor"]
    tokens = P(("groups", "tensor"), None)
    weights = P("tensor", None)
    return jax.shard_map(
        lambda *args: body(size, *args),
        mesh=mesh,
        in_specs=(tokens, tokens, tokens, weights, weights, weights),
        out_specs=tokens,
        check_vma=False,
    )
```

```python
import jax
import jax.numpy as jnp
from jax import lax
from jax.experimental import pallas as pl
from jax.experimental.pallas import tpu as pltpu
from jax.sharding import PartitionSpec as P

CAP = 12
PAIR = 2 * CAP
F32 = jnp.float32
BF16 = jnp.bfloat16
MIB = 2**20


def permutations(size):
    chips = size // 2
    order = list(range(0, chips, 2)) + list(range(chips - 1, 0, -2))

    def pairs(target):
        made = []
        for place, chip in enumerate(order):
            for core in range(2):
                step, to = target(core)
                made.append((2 * chip + core, 2 * order[(place + step) % chips] + to))
        return made

    way = (1, -1)
    return {
        "swap": pairs(lambda core: (0, 1 - core)),
        "one": pairs(lambda core: (way[core], core)),
        "two": pairs(lambda core: (2 * way[core], core)),
        "board": pairs(lambda core: (way[1 - core], 1 - core)),
        "leave": pairs(lambda core: (way[core], 1 - core)),
    }


def choose(ids):
    tokens = ids.shape[1]
    routed = jnp.max(jnp.where(ids == 0, 1.0, 0.0), axis=0, keepdims=True)
    earlier = lax.broadcasted_iota(jnp.int32, (tokens, tokens), 0) < lax.broadcasted_iota(
        jnp.int32, (tokens, tokens), 1
    )
    before = jnp.dot(
        jnp.broadcast_to(routed, (8, tokens)).astype(BF16),
        jnp.where(earlier, 1.0, 0.0).astype(BF16),
        preferred_element_type=F32,
    )[:1]

    def rows(first):
        slot = lax.broadcasted_iota(jnp.int32, (PAIR, tokens), 0) - first
        return jnp.where((slot.astype(F32) == before) & (routed > 0.0), 1.0, 0.0).astype(BF16)

    return rows(0), rows(CAP)


def compact_kernel(ids_ref, tokens_ref, out_ref):
    half = out_ref.shape[1]
    upper, lower = choose(ids_ref[...])
    out_ref[...] = (
        jnp.dot(upper, tokens_ref[:, :half], preferred_element_type=F32)
        + jnp.dot(lower, tokens_ref[:, half:], preferred_element_type=F32)
    ).astype(BF16)


def copy_kernel(in_ref, out_ref):
    out_ref[...] = in_ref[...]


def hidden_kernel(blocks, *refs):
    arrays, (gate_ref, up_ref, out_ref, first, second) = refs[:-5], refs[-5:]
    units, width = gate_ref.shape
    half = width // 2
    for j, (i, row) in enumerate(blocks):
        first[j * CAP : (j + 1) * CAP, :] = arrays[i][row : row + CAP, :]
        second[j * CAP : (j + 1) * CAP, :] = arrays[i][row + CAP : row + PAIR, :]
    contract = (((1,), (1,)), ((), ()))

    def product(ref, here):
        return lax.dot_general(
            first[...], ref[here, :half], contract, preferred_element_type=F32
        ) + lax.dot_general(second[...], ref[here, half:], contract, preferred_element_type=F32)

    tile = 224 if units % 224 == 0 else units
    for start in range(0, units, tile):
        here = slice(start, start + tile)
        gate = product(gate_ref, here)
        up = product(up_ref, here)
        out_ref[:, here] = (gate / (1.0 + jnp.exp(-gate)) * up).astype(BF16)


def down_kernel(places, hidden_ref, down_ref, *out_refs):
    half = down_ref.shape[1] // 2
    tile = half // 3
    for step in range(3):
        here = slice(step * tile, (step + 1) * tile)
        low, high = (
            jnp.dot(
                hidden_ref[...],
                down_ref[:, start + step * tile : start + (step + 1) * tile],
                preferred_element_type=F32,
            )
            for start in (0, half)
        )
        for out_ref, indices in zip(out_refs, places):
            for k, j in enumerate(indices):
                rows = slice(j * CAP, (j + 1) * CAP)
                out_ref[k * PAIR : (k + 1) * PAIR, here] = jnp.concatenate(
                    [low[rows], high[rows]]
                ).astype(out_ref.dtype)


def sum_kernel(blocks, *refs):
    out_ref = refs[-1]
    total = sum(refs[i][row : row + PAIR, :].astype(F32) for i, row in blocks)
    out_ref[...] = total.astype(out_ref.dtype)


def mix_kernel(blocks, ids_ref, gates_ref, *refs):
    (*arrays, out_ref, values, written) = refs
    half = values.shape[1] // 2
    tile = half // 3
    ids = ids_ref[...]
    tokens = ids.shape[1]
    share = jnp.sum(jnp.where(ids == 0, gates_ref[...], 0.0), axis=0, keepdims=True)
    share = jnp.broadcast_to(share, (tokens, tokens)).T[:, :1]
    choosers = choose(ids)
    copies = []
    for step in range(3):
        here = slice(step * tile, (step + 1) * tile)
        rows = sum(arrays[i][row : row + PAIR, here].astype(F32) for i, row in blocks).astype(BF16)
        for side, chooser in enumerate(choosers):
            picked = lax.dot_general(
                chooser, rows, (((0,), (0,)), ((), ())), preferred_element_type=F32
            )
            start = side * half + step * tile
            there = slice(start, start + tile)
            values[:, there] = (share * picked).astype(BF16)
            copies.append(
                pltpu.make_async_copy(
                    values.at[:, there], out_ref.at[:, there], written.at[2 * step + side]
                )
            )
            copies[-1].start()
    for copy in copies:
        copy.wait()


def call(kernel, out_shape, *args, scratch=(), flops=0, **specs):
    moved = sum(a.size * a.dtype.itemsize for a in args)
    return pl.pallas_call(
        kernel,
        out_shape=out_shape,
        scratch_shapes=list(scratch),
        compiler_params=pltpu.CompilerParams(vmem_limit_bytes=16 * MIB),
        cost_estimate=pl.CostEstimate(flops=flops, bytes_accessed=moved, transcendentals=0),
        **specs,
    )(*args)


def distinct(blocks):
    arrays, where = [], []
    for a, row in blocks:
        i = next((i for i, known in enumerate(arrays) if known is a), len(arrays))
        if i == len(arrays):
            arrays.append(a)
        where.append((i, row))
    return arrays, where


def body(size, tokens, expert_ids, gates, gate_weight, up_weight, down_weight):
    count, width = tokens.shape
    half = width // 2
    units = gate_weight.shape[0]
    chips = size // 2
    reach = chips // 2
    rows = size * CAP
    steps = permutations(size)

    def move(kind, a):
        return lax.ppermute(a.astype(BF16), "tensor", steps[kind])

    struct = jax.ShapeDtypeStruct
    ids = expert_ids.T
    work = 2 * rows * units * width
    own = call(compact_kernel, struct((PAIR, half), BF16), ids, tokens)
    own = call(copy_kernel, struct(own.shape, BF16), own, flops=20 * work)

    def block(a, k=0):
        return a, k * PAIR

    def add(blocks):
        arrays, where = distinct(blocks)
        return call(lambda *refs: sum_kernel(where, *refs), struct((PAIR, half), BF16), *arrays)

    behind = {("like", 0): own, ("cross", 0): move("swap", own)}
    for distance in range(1, reach + 1):
        if distance < reach:
            source = behind["cross", distance - 1] if distance > 1 else own
            behind["cross", distance] = move("one" if distance > 1 else "board", source)
        length = 2 - distance % 2
        behind["like", distance] = move("two" if length == 2 else "one", behind["like", distance - length])
    behind["cross", reach] = move("swap", behind["like", reach])
    other = {"like": "cross", "cross": "like"}
    ahead = {
        (other[kind], distance): move("swap", a)
        for (kind, distance), a in behind.items()
        if 0 < distance < reach
    }
    behind, ahead = ({name: block(a) for name, a in found.items()} for found in (behind, ahead))

    names, blocks = {}, []
    for side, found in (("behind", behind), ("ahead", ahead)):
        for kind, distance in found:
            names[side, kind, distance] = len(blocks)
            blocks.append(found[kind, distance])

    arrays, where = distinct(blocks)
    hidden = call(
        lambda *refs: hidden_kernel(where, *refs),
        struct((rows, units), BF16),
        *arrays,
        gate_weight,
        up_weight,
        scratch=[pltpu.VMEM((rows, half), BF16)] * 2,
        flops=2 * work,
    )

    away = range(reach - 1, 0, -1)
    kept = [("like", reach)] + [(kind, d) for d in away for kind in ("like", "cross")] + [("like", 0)]
    def index(kind, distance, side):
        side = "behind" if distance in (0, reach) else side
        return names[side, kind, distance]

    urgent = 3
    places = [
        [index(kind, d, "ahead") for kind, d in kept],
        [index(other[kind], d, "behind") for kind, d in kept[:urgent]],
        [index(other[kind], d, "behind") for kind, d in kept[urgent:]],
    ]
    keep, *sent = call(
        lambda *refs: down_kernel(places, *refs),
        [
            struct((len(indices) * PAIR, half), kind)
            for indices, kind in zip(places, (F32, BF16, BF16))
        ],
        hidden,
        down_weight,
        flops=work,
    )
    urgently = move("swap", sent[0])
    rest, urgently = lax.optimization_barrier((sent[1], urgently))
    sent = [urgently, move("swap", rest)]

    def terms(kind, distance):
        k = kept.index((kind, distance))
        return [block(keep, k), block(sent[0], k) if k < urgent else block(sent[1], k - urgent)]

    came, arrived = {}, []

    def total(kind, distance):
        return add(terms(kind, distance) + came.get((kind, distance), []))

    def deliver(kind, a, name, distance):
        held = came.setdefault((name, distance), []) if distance else arrived
        held.append(block(move(kind, a)))

    first = [("cross", reach - 1), ("like", reach), ("like", reach - 1)]
    ready = dict(zip(first, lax.optimization_barrier(tuple(total(*name) for name in first))))
    deliver("one", ready["cross", reach - 1], "cross", reach - 2)
    deliver("two", ready["like", reach], "like", reach - 2)
    deliver("one", ready["like", reach - 1], "like", reach - 2)
    for distance in range(reach - 2, 0, -1):
        cross = total("cross", distance)
        if distance == 1:
            deliver("leave", cross, "like", 0)
        elif distance == 2:
            cross, near = lax.optimization_barrier((cross, total("like", 1)))
            deliver("one", cross, "cross", 1)
            deliver("one", near, "like", 0)
            deliver("two", total("like", 2), "like", 0)
        elif distance % 2:
            deliver("one", cross, "cross", distance - 1)
            deliver("one", total("like", distance), "like", distance - 1)
        else:
            deliver("one", cross, "cross", distance - 1)
            deliver("two", total("like", distance), "like", distance - 2)
    arrays, mixed = distinct(arrived + terms("like", 0))
    return call(
        lambda *refs: mix_kernel(mixed, *refs),
        struct(tokens.shape, BF16),
        ids,
        gates.T,
        *arrays,
        out_specs=pl.BlockSpec(memory_space=pl.ANY),
        scratch=[pltpu.VMEM(tokens.shape, BF16), pltpu.SemaphoreType.DMA((6,))],
    )


def solution(mesh):
    size = mesh.shape["tensor"]
    tokens = P(("groups", "tensor"), None)
    weights = P("tensor", None)
    return jax.shard_map(
        lambda *args: body(size, *args),
        mesh=mesh,
        in_specs=(tokens, tokens, tokens, weights, weights, weights),
        out_specs=tokens,
        check_vma=False,
    )
```

```python
import jax
import jax.numpy as jnp
from jax import lax
from jax.experimental import pallas as pl
from jax.experimental.pallas import tpu as pltpu
from jax.sharding import PartitionSpec as P

CAP = 12
PAIR = 2 * CAP
F32 = jnp.float32
BF16 = jnp.bfloat16
MIB = 2**20


def permutations(size):
    chips = size // 2
    order = list(range(0, chips, 2)) + list(range(chips - 1, 0, -2))

    def pairs(target):
        made = []
        for place, chip in enumerate(order):
            for core in range(2):
                step, to = target(core)
                made.append((2 * chip + core, 2 * order[(place + step) % chips] + to))
        return made

    way = (1, -1)
    return {
        "swap": pairs(lambda core: (0, 1 - core)),
        "one": pairs(lambda core: (way[core], core)),
        "two": pairs(lambda core: (2 * way[core], core)),
        "board": pairs(lambda core: (way[1 - core], 1 - core)),
        "leave": pairs(lambda core: (way[core], 1 - core)),
    }


def choose(ids):
    tokens = ids.shape[1]
    routed = jnp.max(jnp.where(ids == 0, 1.0, 0.0), axis=0, keepdims=True)
    earlier = lax.broadcasted_iota(jnp.int32, (tokens, tokens), 0) < lax.broadcasted_iota(
        jnp.int32, (tokens, tokens), 1
    )
    before = jnp.dot(
        jnp.broadcast_to(routed, (8, tokens)).astype(BF16),
        jnp.where(earlier, 1.0, 0.0).astype(BF16),
        preferred_element_type=F32,
    )[:1]

    def rows(first):
        slot = lax.broadcasted_iota(jnp.int32, (PAIR, tokens), 0) - first
        return jnp.where((slot.astype(F32) == before) & (routed > 0.0), 1.0, 0.0).astype(BF16)

    return rows(0), rows(CAP)


def compact_kernel(ids_ref, tokens_ref, out_ref, upper_ref, lower_ref, ids_here, tokens_here, arrived):
    half = out_ref.shape[1]
    tile = half // 3
    copies = [pltpu.make_async_copy(ids_ref, ids_here, arrived.at[6])]
    for step in range(3):
        for side in range(2):
            start = side * half + step * tile
            there = slice(start, start + tile)
            copies.append(
                pltpu.make_async_copy(
                    tokens_ref.at[:, there], tokens_here.at[:, there], arrived.at[2 * step + side]
                )
            )
    for copy in copies:
        copy.start()
    copies[0].wait()
    choosers = choose(ids_here[...])
    upper_ref[...], lower_ref[...] = choosers
    for step in range(3):
        here = slice(step * tile, (step + 1) * tile)
        total = 0.0
        for side, chooser in enumerate(choosers):
            copies[1 + 2 * step + side].wait()
            start = side * half + step * tile
            total = total + jnp.dot(
                chooser, tokens_here[:, start : start + tile], preferred_element_type=F32
            )
        out_ref[:, here] = total.astype(BF16)


def copy_kernel(in_ref, out_ref):
    out_ref[...] = in_ref[...]


def hidden_kernel(blocks, *refs):
    arrays, (gate_ref, up_ref, out_ref, first, second) = refs[:-5], refs[-5:]
    units, width = gate_ref.shape
    half = width // 2
    for j, (i, row) in enumerate(blocks):
        first[j * CAP : (j + 1) * CAP, :] = arrays[i][row : row + CAP, :]
        second[j * CAP : (j + 1) * CAP, :] = arrays[i][row + CAP : row + PAIR, :]
    contract = (((1,), (1,)), ((), ()))

    def product(ref, here):
        return lax.dot_general(
            first[...], ref[here, :half], contract, preferred_element_type=F32
        ) + lax.dot_general(second[...], ref[here, half:], contract, preferred_element_type=F32)

    tile = 224 if units % 224 == 0 else units
    for start in range(0, units, tile):
        here = slice(start, start + tile)
        gate = product(gate_ref, here)
        up = product(up_ref, here)
        out_ref[:, here] = (gate / (1.0 + jnp.exp(-gate)) * up).astype(BF16)


def down_kernel(places, hidden_ref, down_ref, *out_refs):
    half = down_ref.shape[1] // 2
    tile = half // 3
    for step in range(3):
        here = slice(step * tile, (step + 1) * tile)
        low, high = (
            jnp.dot(
                hidden_ref[...],
                down_ref[:, start + step * tile : start + (step + 1) * tile],
                preferred_element_type=F32,
            )
            for start in (0, half)
        )
        for out_ref, indices in zip(out_refs, places):
            for k, j in enumerate(indices):
                rows = slice(j * CAP, (j + 1) * CAP)
                out_ref[k * PAIR : (k + 1) * PAIR, here] = jnp.concatenate(
                    [low[rows], high[rows]]
                ).astype(out_ref.dtype)


def sum_kernel(blocks, *refs):
    out_ref = refs[-1]
    total = sum(refs[i][row : row + PAIR, :].astype(F32) for i, row in blocks)
    out_ref[...] = total.astype(out_ref.dtype)


def mix_kernel(blocks, ids_ref, gates_ref, upper_ref, lower_ref, *refs):
    (*arrays, out_ref, values, written) = refs
    half = values.shape[1] // 2
    tile = half // 3
    ids = ids_ref[...]
    tokens = ids.shape[1]
    share = jnp.sum(jnp.where(ids == 0, gates_ref[...], 0.0), axis=0, keepdims=True)
    share = jnp.broadcast_to(share, (tokens, tokens)).T[:, :1]
    choosers = (upper_ref[...], lower_ref[...])
    copies = []
    for step in range(3):
        here = slice(step * tile, (step + 1) * tile)
        rows = sum(arrays[i][row : row + PAIR, here].astype(F32) for i, row in blocks).astype(BF16)
        for side, chooser in enumerate(choosers):
            picked = lax.dot_general(
                chooser, rows, (((0,), (0,)), ((), ())), preferred_element_type=F32
            )
            start = side * half + step * tile
            there = slice(start, start + tile)
            values[:, there] = (share * picked).astype(BF16)
            copies.append(
                pltpu.make_async_copy(
                    values.at[:, there], out_ref.at[:, there], written.at[2 * step + side]
                )
            )
            copies[-1].start()
    for copy in copies:
        copy.wait()


def call(kernel, out_shape, *args, scratch=(), flops=0, **specs):
    moved = sum(a.size * a.dtype.itemsize for a in args)
    return pl.pallas_call(
        kernel,
        out_shape=out_shape,
        scratch_shapes=list(scratch),
        compiler_params=pltpu.CompilerParams(vmem_limit_bytes=16 * MIB),
        cost_estimate=pl.CostEstimate(flops=flops, bytes_accessed=moved, transcendentals=0),
        **specs,
    )(*args)


def distinct(blocks):
    arrays, where = [], []
    for a, row in blocks:
        i = next((i for i, known in enumerate(arrays) if known is a), len(arrays))
        if i == len(arrays):
            arrays.append(a)
        where.append((i, row))
    return arrays, where


def body(size, tokens, expert_ids, gates, gate_weight, up_weight, down_weight):
    count, width = tokens.shape
    half = width // 2
    units = gate_weight.shape[0]
    chips = size // 2
    reach = chips // 2
    rows = size * CAP
    steps = permutations(size)

    def move(kind, a):
        return lax.ppermute(a.astype(BF16), "tensor", steps[kind])

    struct = jax.ShapeDtypeStruct
    ids = expert_ids.T
    work = 2 * rows * units * width
    own, *choosers = call(
        compact_kernel,
        [struct((PAIR, half), BF16)] + [struct((PAIR, count), BF16)] * 2,
        pltpu.with_memory_space_constraint(ids, pltpu.MemorySpace.HBM),
        pltpu.with_memory_space_constraint(tokens, pltpu.MemorySpace.HBM),
        in_specs=[pl.BlockSpec(memory_space=pl.ANY)] * 2,
        scratch=[
            pltpu.VMEM(ids.shape, ids.dtype),
            pltpu.VMEM(tokens.shape, BF16),
            pltpu.SemaphoreType.DMA((7,)),
        ],
    )
    own = call(copy_kernel, struct(own.shape, BF16), own, flops=8 * work)

    def block(a, k=0):
        return a, k * PAIR

    def add(blocks):
        arrays, where = distinct(blocks)
        return call(lambda *refs: sum_kernel(where, *refs), struct((PAIR, half), BF16), *arrays)

    behind = {("like", 0): own, ("cross", 0): move("swap", own)}
    for distance in range(1, reach + 1):
        if distance < reach:
            source = behind["cross", distance - 1] if distance > 1 else own
            behind["cross", distance] = move("one" if distance > 1 else "board", source)
        length = 2 - distance % 2
        behind["like", distance] = move("two" if length == 2 else "one", behind["like", distance - length])
    behind["cross", reach] = move("swap", behind["like", reach])
    other = {"like": "cross", "cross": "like"}
    ahead = {
        (other[kind], distance): move("swap", a)
        for (kind, distance), a in behind.items()
        if 0 < distance < reach
    }
    behind, ahead = ({name: block(a) for name, a in found.items()} for found in (behind, ahead))

    names, blocks = {}, []
    for side, found in (("behind", behind), ("ahead", ahead)):
        for kind, distance in found:
            names[side, kind, distance] = len(blocks)
            blocks.append(found[kind, distance])

    arrays, where = distinct(blocks)
    hidden = call(
        lambda *refs: hidden_kernel(where, *refs),
        struct((rows, units), BF16),
        *arrays,
        gate_weight,
        up_weight,
        scratch=[pltpu.VMEM((rows, half), BF16)] * 2,
        flops=2 * work,
    )

    away = range(reach - 1, 0, -1)
    kept = [("like", reach)] + [(kind, d) for d in away for kind in ("like", "cross")] + [("like", 0)]
    def index(kind, distance, side):
        side = "behind" if distance in (0, reach) else side
        return names[side, kind, distance]

    urgent = 3
    places = [
        [index(kind, d, "ahead") for kind, d in kept],
        [index(other[kind], d, "behind") for kind, d in kept[:urgent]],
        [index(other[kind], d, "behind") for kind, d in kept[urgent:]],
    ]
    keep, *sent = call(
        lambda *refs: down_kernel(places, *refs),
        [
            struct((len(indices) * PAIR, half), kind)
            for indices, kind in zip(places, (F32, BF16, BF16))
        ],
        hidden,
        down_weight,
        flops=work,
    )
    urgently = move("swap", sent[0])
    rest, urgently = lax.optimization_barrier((sent[1], urgently))
    sent = [urgently, move("swap", rest)]

    def terms(kind, distance):
        k = kept.index((kind, distance))
        return [block(keep, k), block(sent[0], k) if k < urgent else block(sent[1], k - urgent)]

    came, arrived = {}, []

    def total(kind, distance):
        return add(terms(kind, distance) + came.get((kind, distance), []))

    def deliver(kind, a, name, distance):
        held = came.setdefault((name, distance), []) if distance else arrived
        held.append(block(move(kind, a)))

    first = [("cross", reach - 1), ("like", reach), ("like", reach - 1)]
    ready = dict(zip(first, lax.optimization_barrier(tuple(total(*name) for name in first))))
    deliver("one", ready["cross", reach - 1], "cross", reach - 2)
    deliver("two", ready["like", reach], "like", reach - 2)
    deliver("one", ready["like", reach - 1], "like", reach - 2)
    for distance in range(reach - 2, 0, -1):
        cross = total("cross", distance)
        if distance == 1:
            deliver("leave", cross, "like", 0)
        elif distance == 2:
            cross, near = lax.optimization_barrier((cross, total("like", 1)))
            deliver("one", cross, "cross", 1)
            deliver("one", near, "like", 0)
            deliver("two", total("like", 2), "like", 0)
        elif distance % 2:
            deliver("one", cross, "cross", distance - 1)
            deliver("one", total("like", distance), "like", distance - 1)
        else:
            deliver("one", cross, "cross", distance - 1)
            deliver("two", total("like", distance), "like", distance - 2)
    arrays, mixed = distinct(arrived + terms("like", 0))
    return call(
        lambda *refs: mix_kernel(mixed, *refs),
        struct(tokens.shape, BF16),
        ids,
        gates.T,
        *choosers,
        *arrays,
        out_specs=pl.BlockSpec(memory_space=pl.ANY),
        scratch=[pltpu.VMEM(tokens.shape, BF16), pltpu.SemaphoreType.DMA((6,))],
    )


def solution(mesh):
    size = mesh.shape["tensor"]
    tokens = P(("groups", "tensor"), None)
    weights = P("tensor", None)
    return jax.shard_map(
        lambda *args: body(size, *args),
        mesh=mesh,
        in_specs=(tokens, tokens, tokens, weights, weights, weights),
        out_specs=tokens,
        check_vma=False,
    )
```

```python
import jax
import jax.numpy as jnp
from jax import lax
from jax.experimental import pallas as pl
from jax.experimental.pallas import tpu as pltpu
from jax.sharding import PartitionSpec as P

CAP = 12
PAIR = 2 * CAP
F32 = jnp.float32
BF16 = jnp.bfloat16
MIB = 2**20


def permutations(size):
    chips = size // 2
    order = list(range(0, chips, 2)) + list(range(chips - 1, 0, -2))

    def pairs(target):
        made = []
        for place, chip in enumerate(order):
            for core in range(2):
                step, to = target(core)
                made.append((2 * chip + core, 2 * order[(place + step) % chips] + to))
        return made

    way = (1, -1)
    return {
        "swap": pairs(lambda core: (0, 1 - core)),
        "one": pairs(lambda core: (way[core], core)),
        "two": pairs(lambda core: (2 * way[core], core)),
        "board": pairs(lambda core: (way[1 - core], 1 - core)),
        "leave": pairs(lambda core: (way[core], 1 - core)),
    }


def choose(ids):
    tokens = ids.shape[1]
    routed = jnp.max(jnp.where(ids == 0, 1.0, 0.0), axis=0, keepdims=True)
    earlier = lax.broadcasted_iota(jnp.int32, (tokens, tokens), 0) < lax.broadcasted_iota(
        jnp.int32, (tokens, tokens), 1
    )
    before = jnp.dot(
        jnp.broadcast_to(routed, (8, tokens)).astype(BF16),
        jnp.where(earlier, 1.0, 0.0).astype(BF16),
        preferred_element_type=F32,
    )[:1]

    def rows(first):
        slot = lax.broadcasted_iota(jnp.int32, (PAIR, tokens), 0) - first
        return jnp.where((slot.astype(F32) == before) & (routed > 0.0), 1.0, 0.0).astype(BF16)

    return rows(0), rows(CAP)


def compact_kernel(ids_ref, tokens_ref, out_ref, upper_ref, lower_ref, ids_here, tokens_here, arrived):
    half = out_ref.shape[1]
    tile = half // 3
    copies = [pltpu.make_async_copy(ids_ref, ids_here, arrived.at[6])]
    for step in range(3):
        for side in range(2):
            start = side * half + step * tile
            there = slice(start, start + tile)
            copies.append(
                pltpu.make_async_copy(
                    tokens_ref.at[:, there], tokens_here.at[:, there], arrived.at[2 * step + side]
                )
            )
    for copy in copies:
        copy.start(priority=1)
    copies[0].wait()
    choosers = choose(ids_here[...])
    upper_ref[...], lower_ref[...] = choosers
    for step in range(3):
        here = slice(step * tile, (step + 1) * tile)
        total = 0.0
        for side, chooser in enumerate(choosers):
            copies[1 + 2 * step + side].wait()
            start = side * half + step * tile
            total = total + jnp.dot(
                chooser, tokens_here[:, start : start + tile], preferred_element_type=F32
            )
        out_ref[:, here] = total.astype(BF16)


def copy_kernel(in_ref, out_ref):
    out_ref[...] = in_ref[...]


def share_kernel(ids_ref, gates_ref, out_ref):
    share = jnp.sum(jnp.where(ids_ref[...] == 0, gates_ref[...], 0.0), axis=0, keepdims=True)
    out_ref[...] = jnp.broadcast_to(share, out_ref.shape).T


def hidden_kernel(blocks, *refs):
    arrays, (gate_ref, up_ref, out_ref, first, second) = refs[:-5], refs[-5:]
    half = gate_ref.shape[1] // 2
    for j, (i, row) in enumerate(blocks):
        first[j * CAP : (j + 1) * CAP, :] = arrays[i][row : row + CAP, :]
        second[j * CAP : (j + 1) * CAP, :] = arrays[i][row + CAP : row + PAIR, :]
    contract = (((1,), (1,)), ((), ()))

    def product(ref):
        return lax.dot_general(
            first[...], ref[:, :half], contract, preferred_element_type=F32
        ) + lax.dot_general(second[...], ref[:, half:], contract, preferred_element_type=F32)

    gate = product(gate_ref)
    up = product(up_ref)
    out_ref[...] = (gate / (1.0 + jnp.exp(-gate)) * up).astype(BF16)


def down_kernel(places, hidden_ref, down_ref, *out_refs):
    half = down_ref.shape[1] // 2
    tile = half // 3
    for step in range(3):
        here = slice(step * tile, (step + 1) * tile)
        low, high = (
            jnp.dot(
                hidden_ref[...],
                down_ref[:, start + step * tile : start + (step + 1) * tile],
                preferred_element_type=F32,
            )
            for start in (0, half)
        )
        for out_ref, indices in zip(out_refs, places):
            for k, j in enumerate(indices):
                rows = slice(j * CAP, (j + 1) * CAP)
                out_ref[k * PAIR : (k + 1) * PAIR, here] = jnp.concatenate(
                    [low[rows], high[rows]]
                ).astype(out_ref.dtype)


def sum_kernel(blocks, *refs):
    out_ref = refs[-1]
    total = sum(refs[i][row : row + PAIR, :].astype(F32) for i, row in blocks)
    out_ref[...] = total.astype(out_ref.dtype)


def mix_kernel(blocks, share_ref, upper_ref, lower_ref, *refs):
    (*arrays, out_ref, values, written) = refs
    half = values.shape[1] // 2
    tile = half // 3
    share = share_ref[:, :1]
    choosers = (upper_ref[...], lower_ref[...])
    copies = []
    for step in range(3):
        here = slice(step * tile, (step + 1) * tile)
        rows = sum(arrays[i][row : row + PAIR, here].astype(F32) for i, row in blocks).astype(BF16)
        for side, chooser in enumerate(choosers):
            picked = lax.dot_general(
                chooser, rows, (((0,), (0,)), ((), ())), preferred_element_type=F32
            )
            start = side * half + step * tile
            there = slice(start, start + tile)
            values[:, there] = (share * picked).astype(BF16)
            copies.append(
                pltpu.make_async_copy(
                    values.at[:, there], out_ref.at[:, there], written.at[2 * step + side]
                )
            )
            copies[-1].start()
    for copy in copies:
        copy.wait()


def call(kernel, out_shape, *args, scratch=(), flops=0, **specs):
    moved = sum(a.size * a.dtype.itemsize for a in args)
    return pl.pallas_call(
        kernel,
        out_shape=out_shape,
        scratch_shapes=list(scratch),
        compiler_params=pltpu.CompilerParams(vmem_limit_bytes=16 * MIB),
        cost_estimate=pl.CostEstimate(flops=flops, bytes_accessed=moved, transcendentals=0),
        **specs,
    )(*args)


def distinct(blocks):
    arrays, where = [], []
    for a, row in blocks:
        i = next((i for i, known in enumerate(arrays) if known is a), len(arrays))
        if i == len(arrays):
            arrays.append(a)
        where.append((i, row))
    return arrays, where


def body(size, tokens, expert_ids, gates, gate_weight, up_weight, down_weight):
    count, width = tokens.shape
    half = width // 2
    units = gate_weight.shape[0]
    chips = size // 2
    reach = chips // 2
    rows = size * CAP
    steps = permutations(size)

    def move(kind, a):
        return lax.ppermute(a.astype(BF16), "tensor", steps[kind])

    struct = jax.ShapeDtypeStruct
    ids = expert_ids.T
    work = 2 * rows * units * width
    own, *choosers = call(
        compact_kernel,
        [struct((PAIR, half), BF16)] + [struct((PAIR, count), BF16)] * 2,
        pltpu.with_memory_space_constraint(ids, pltpu.MemorySpace.HBM),
        pltpu.with_memory_space_constraint(tokens, pltpu.MemorySpace.HBM),
        in_specs=[pl.BlockSpec(memory_space=pl.ANY)] * 2,
        scratch=[
            pltpu.VMEM(ids.shape, ids.dtype),
            pltpu.VMEM(tokens.shape, BF16),
            pltpu.SemaphoreType.DMA((7,)),
        ],
    )
    own = call(copy_kernel, struct(own.shape, BF16), own, flops=8 * work)

    def block(a, k=0):
        return a, k * PAIR

    def add(blocks):
        arrays, where = distinct(blocks)
        return call(lambda *refs: sum_kernel(where, *refs), struct((PAIR, half), BF16), *arrays)

    behind = {("like", 0): own, ("cross", 0): move("swap", own)}
    for distance in range(1, reach + 1):
        if distance < reach:
            source = behind["cross", distance - 1] if distance > 1 else own
            behind["cross", distance] = move("one" if distance > 1 else "board", source)
        length = 2 - distance % 2
        behind["like", distance] = move("two" if length == 2 else "one", behind["like", distance - length])
    behind["cross", reach] = move("swap", behind["like", reach])
    other = {"like": "cross", "cross": "like"}
    ahead = {
        (other[kind], distance): move("swap", a)
        for (kind, distance), a in behind.items()
        if 0 < distance < reach
    }
    behind, ahead = ({name: block(a) for name, a in found.items()} for found in (behind, ahead))

    names, blocks = {}, []
    for side, found in (("behind", behind), ("ahead", ahead)):
        for kind, distance in found:
            names[side, kind, distance] = len(blocks)
            blocks.append(found[kind, distance])

    arrays, where = distinct(blocks)
    share = call(share_kernel, struct((count, count), F32), ids, gates.T)
    hidden = call(
        lambda *refs: hidden_kernel(where, *refs),
        struct((rows, units), BF16),
        *arrays,
        gate_weight,
        up_weight,
        scratch=[pltpu.VMEM((rows, half), BF16)] * 2,
        flops=2 * work,
    )

    away = range(reach - 1, 0, -1)
    kept = [("like", reach)] + [(kind, d) for d in away for kind in ("like", "cross")] + [("like", 0)]
    def index(kind, distance, side):
        side = "behind" if distance in (0, reach) else side
        return names[side, kind, distance]

    urgent = 3
    places = [
        [index(kind, d, "ahead") for kind, d in kept],
        [index(other[kind], d, "behind") for kind, d in kept[:urgent]],
        [index(other[kind], d, "behind") for kind, d in kept[urgent:]],
    ]
    keep, *sent = call(
        lambda *refs: down_kernel(places, *refs),
        [
            struct((len(indices) * PAIR, half), kind)
            for indices, kind in zip(places, (F32, BF16, BF16))
        ],
        hidden,
        down_weight,
        flops=work,
    )
    urgently = move("swap", sent[0])
    rest, urgently = lax.optimization_barrier((sent[1], urgently))
    sent = [urgently, move("swap", rest)]

    def terms(kind, distance):
        k = kept.index((kind, distance))
        return [block(keep, k), block(sent[0], k) if k < urgent else block(sent[1], k - urgent)]

    came, arrived = {}, []

    def total(kind, distance):
        return add(terms(kind, distance) + came.get((kind, distance), []))

    def deliver(kind, a, name, distance):
        held = came.setdefault((name, distance), []) if distance else arrived
        held.append(block(move(kind, a)))

    first = [("cross", reach - 1), ("like", reach), ("like", reach - 1)]
    ready = dict(zip(first, lax.optimization_barrier(tuple(total(*name) for name in first))))
    deliver("one", ready["cross", reach - 1], "cross", reach - 2)
    deliver("two", ready["like", reach], "like", reach - 2)
    deliver("one", ready["like", reach - 1], "like", reach - 2)
    for distance in range(reach - 2, 0, -1):
        cross = total("cross", distance)
        if distance == 1:
            deliver("leave", cross, "like", 0)
        elif distance == 2:
            cross, near = lax.optimization_barrier((cross, total("like", 1)))
            deliver("one", cross, "cross", 1)
            deliver("one", near, "like", 0)
            deliver("two", total("like", 2), "like", 0)
        elif distance % 2:
            deliver("one", cross, "cross", distance - 1)
            deliver("one", total("like", distance), "like", distance - 1)
        else:
            deliver("one", cross, "cross", distance - 1)
            deliver("two", total("like", distance), "like", distance - 2)
    early = arrived[:1] + terms("like", 0)
    arrays, where = distinct(early)
    early = call(lambda *refs: sum_kernel(where, *refs), struct((PAIR, half), F32), *arrays)
    arrays, mixed = distinct(arrived[1:] + [block(early)])
    return call(
        lambda *refs: mix_kernel(mixed, *refs),
        struct(tokens.shape, BF16),
        share,
        *choosers,
        *arrays,
        out_specs=pl.BlockSpec(memory_space=pl.ANY),
        scratch=[pltpu.VMEM(tokens.shape, BF16), pltpu.SemaphoreType.DMA((6,))],
    )


def solution(mesh):
    size = mesh.shape["tensor"]
    tokens = P(("groups", "tensor"), None)
    weights = P("tensor", None)
    return jax.shard_map(
        lambda *args: body(size, *args),
        mesh=mesh,
        in_specs=(tokens, tokens, tokens, weights, weights, weights),
        out_specs=tokens,
        check_vma=False,
    )
```
